32 devices in a mesh: groups: 2 (over y), rows: 4 (over z), sub: 2 (over x), rep: 2 (over core).
Axes of the slice: x: 2, y: 2, z: 4, core: 2. Of those that a mesh axis runs over, the one named last changes fastest.
Arguments:
- queries: float32 [256, 8192], P('rep', ('groups', 'rows', 'sub')), parts along dimension 1, may hold values from -10.5 to 10.5
- tiles: bfloat16 [128, 512, 512], P(('groups', 'rows', 'sub')), parts along dimension 0, may hold values from 0.01 to 10, as said below
- pair_blocks: int32 [128, 2], P('groups'), parts along dimension 0, may hold values from 0 to 7, as said below
Outputs:
- solution: float32 [256, 8192], P('rep', ('groups', 'rows', 'sub')), parts along dimension 1
- residual: float32 [256, 8192], P('rep', ('groups', 'rows', 'sub')), parts along dimension 1
The draws below stay inside these ranges and needn't reach their ends.
There are 2 independent parts, one for each index of `groups`. The reference program is written for one: setup_inputs(seed, part) draws one part's arguments, and reference() takes and returns one part's arrays. A program takes and returns all parts, laid end to end along the dimension named above; each array names one. Nothing has to cross between parts.
Inputs may be any that keep to these rules, and one draw needn't show every extreme that they name: `pair_blocks`: row t describes tile t. Tiles 8 * b to 8 * b + 7 belong to block b, and the first of them is (b, b). Every tile of block b has a row block in the same set as b (same value of block // 2) and a column block no smaller than its row block, whose set lies less than 3 sets after b's. The tiles of one block name at most one column block in each later set. `tiles`: positive affinities.
All inputs are finite; a program needn't handle non-finite values.
Results may differ from the reference program's by a relative error of at most 0.01045.
Values may be sent and summed in bfloat16 or wider, within the bound.
A program may use at most 64 MiB of HBM per device.

```python
import jax
import jax.numpy as jnp
from jax import lax

BLOCK = 512
QUERIES = 256
TILE_DEV = 8
SPAN = 3
ITERS = 3
BLOCKS = 8
N_ROWS = 4
N_SUB = 2


def draw_queries(key, part):
    key = jax.random.fold_in(key, 7)
    position = jnp.arange(BLOCKS * BLOCK, dtype=jnp.float32) / (BLOCKS * BLOCK)
    rising = 1.0 + 2.0 * position
    values = jnp.clip(jax.random.normal(key, (QUERIES, BLOCKS * BLOCK)), -3.5, 3.5) * rising
    return values.astype(jnp.float32)


def draw_tiles(key, part):
    key = jax.random.fold_in(key, 5)
    value_key = jax.random.fold_in(key, 0)
    shape = (TILE_DEV * BLOCKS, BLOCK, BLOCK)
    exponent = jax.random.uniform(value_key, shape, minval=-3.0, maxval=0.0)
    values = jnp.exp(exponent)
    return values.astype(jnp.bfloat16)


def draw_pair_blocks(key, part):
    key = jax.random.fold_in(key, 11)
    dist_key, target_key, first_key, second_key = jax.random.split(key, 4)
    block_ids = jnp.arange(BLOCKS, dtype=jnp.int32)
    set_index = block_ids // N_SUB
    distance = jax.random.randint(dist_key, (BLOCKS, TILE_DEV), 0, SPAN)
    distance = distance.at[:, 1].set(1).at[:, 2].set(SPAN - 1)
    distance = jnp.where(set_index[:, None] + distance < N_ROWS, distance, 0)
    distance = distance.at[:, 0].set(0)
    targets = jax.random.randint(target_key, (BLOCKS, SPAN), 0, N_SUB)
    first = jax.random.randint(first_key, (BLOCKS, TILE_DEV), 0, N_SUB)
    second = jax.random.randint(second_key, (BLOCKS, TILE_DEV), 0, N_SUB)
    lower = jnp.minimum(first, second)
    upper = jnp.maximum(first, second)
    base = (set_index * N_SUB)[:, None]
    remote_col = (set_index[:, None] + distance) * N_SUB + jnp.take_along_axis(targets, distance, axis=1)
    row_block = jnp.where(distance == 0, base + lower, base + first)
    col_block = jnp.where(distance == 0, base + upper, remote_col)
    row_block = row_block.at[:, 0].set(block_ids)
    col_block = col_block.at[:, 0].set(block_ids)
    return jnp.stack([row_block, col_block], axis=-1).reshape(TILE_DEV * BLOCKS, 2).astype(jnp.int32)


def setup_inputs(seed: int = 0, part: int = 0) -> dict:
    key_of = jax.random.split(jax.random.key(seed), 4)
    part_splits = jax.random.split(jax.random.fold_in(key_of[3], part), 4)
    return {
        "queries": draw_queries(jax.random.fold_in(jax.random.fold_in(key_of[3], part), 71), part),
        "tiles": draw_tiles(jax.random.fold_in(jax.random.fold_in(key_of[3], part), 71), part),
        "pair_blocks": draw_pair_blocks(jax.random.fold_in(jax.random.fold_in(key_of[3], part), 71), part),
    }


DAMPING = 0.9

def graph_product(row_panel, tiles, pair_blocks):
    columns = row_panel.shape[0]
    blocks = row_panel.reshape(columns, BLOCKS, BLOCK).transpose(1, 0, 2)
    tile_groups = tiles.reshape(BLOCKS, TILE_DEV, BLOCK, BLOCK)
    pair_groups = pair_blocks.reshape(BLOCKS, TILE_DEV, 2)

    def add_group(summed, group_item):
        tile_group, pair_group = group_item
        left_tiles = tile_group.astype(jnp.float32)
        row_inputs = blocks[pair_group[:, 0]].astype(jnp.float32)
        col_inputs = blocks[pair_group[:, 1]].astype(jnp.float32)
        forward = jnp.einsum('tab,tqb->tqa', left_tiles, col_inputs, precision=lax.Precision.HIGHEST)
        backward = jnp.einsum('tab,tqa->tqb', left_tiles, row_inputs, precision=lax.Precision.HIGHEST)
        summed = summed.at[pair_group[:, 0]].add(forward)
        summed = summed.at[pair_group[:, 1]].add(backward)
        return (summed, None)
    start_sum = jnp.zeros((BLOCKS, columns, BLOCK), jnp.float32)
    summed, _ = lax.scan(add_group, start_sum, (tile_groups, pair_groups))
    return summed.transpose(1, 0, 2).reshape(columns, BLOCKS * BLOCK)

def reference(queries, tiles, pair_blocks):
    unit_panel = jnp.ones((1, BLOCKS * BLOCK), jnp.bfloat16)
    degree = graph_product(unit_panel, tiles, pair_blocks)
    inverse_root = 1.0 / jnp.sqrt(degree)

    def operate(field):
        scaled = (inverse_root * field).astype(jnp.bfloat16)
        return field - DAMPING * inverse_root * graph_product(scaled, tiles, pair_blocks)
    solution = jnp.zeros_like(queries)
    residual = queries
    direction = queries
    norm_now = lax.optimization_barrier(jnp.sum(residual * residual, axis=1))
    for iteration in range(ITERS):
        mapped = operate(direction)
        step_size = (norm_now / lax.optimization_barrier(jnp.sum(direction * mapped, axis=1)))[:, None]
        solution = solution + step_size * direction
        residual = residual - step_size * mapped
        norm_next = lax.optimization_barrier(jnp.sum(residual * residual, axis=1))
        direction = residual + (norm_next / norm_now)[:, None] * direction
        norm_now = norm_next
    return (solution, residual)
```

```python
import functools

import jax
import jax.numpy as jnp
from jax import lax
from jax.experimental import pallas as pl
from jax.experimental.pallas import tpu as pltpu
from jax.sharding import PartitionSpec as P

SPAN = 3
ITERS = 3
DAMPING = 0.9
FAR = SPAN - 1
BASIS = ITERS + 1
CHUNKS = 2
MESH = pl.DeviceIdType.MESH
PAIRS = [(i, j) for i in range(BASIS) for j in range(i, BASIS)]


def plain(left, right):
    return jnp.dot(left, right, preferred_element_type=jnp.float32)


def turned(left, right):
    return lax.dot_general(
        left, right, (((1,), (1,)), ((), ())), preferred_element_type=jnp.float32
    )


def flag(condition):
    return jnp.where(condition, 1.0, 0.0).astype(jnp.float32)


def step_coefficients(gram):
    def inner(first, second):
        total = None
        for i in range(BASIS):
            for j in range(BASIS):
                if first[i] is None or second[j] is None:
                    continue
                term = first[i] * second[j] * gram[(min(i, j), max(i, j))]
                total = term if total is None else total + term
        return total

    def plus(first, factor, second):
        out = []
        for a, b in zip(first, second):
            if b is None:
                out.append(a)
            elif a is None:
                out.append(factor * b)
            else:
                out.append(a + factor * b)
        return out

    def mapped_of(vector):
        out = []
        for k in range(BASIS):
            low = vector[k - 1] if k else None
            if low is None:
                out.append(vector[k])
            elif vector[k] is None:
                out.append(-DAMPING * low)
            else:
                out.append(vector[k] - DAMPING * low)
        return out

    one = jnp.ones_like(gram[(0, 0)])
    found = [None] * BASIS
    residual = [one] + [None] * ITERS
    direction = list(residual)
    norm_now = gram[(0, 0)]
    for _ in range(ITERS):
        mapped = mapped_of(direction)
        step = norm_now / inner(direction, mapped)
        found = plus(found, step, direction)
        residual = plus(residual, -step, mapped)
        norm_next = inner(residual, residual)
        direction = plus(residual, norm_next / norm_now, direction)
        norm_now = norm_next
    return found, residual


def kernel(
    rows, sub, pairs, queries, tiles, found_out, residual_out,
    slots, panel, payload, fetched, back_out, back_in, acc, x_out, x_in, means, fields,
    deg_z, deg_z_in, deg_x, deg_x_in, row_sums, gram_all,
    panel_s, panel_r, pay_s, pay_r, back_s, back_r, x_s, x_r, mean_s, mean_r,
    dz_s, dz_r, dx_s, dx_r, gram_s, gram_r,
):
    r = lax.axis_index("rows")
    s = lax.axis_index("sub")
    count = rows * sub
    me = r * sub + s
    tile_count, order, _ = tiles.shape
    columns = queries.shape[0]
    own_slots = [(n, m) for n in range(sub) for m in range(n, sub)]
    slot_of = {pair: k for k, pair in enumerate(own_slots)}
    first_far = len(own_slots)

    def far_slot(n, off):
        return first_far + n * FAR + off - 1

    def device(row, column):
        return {"rows": row, "sub": column}

    for landing in (fetched, back_in, means, deg_z_in, deg_z, deg_x):
        landing[...] = jnp.zeros_like(landing)

    barrier = pltpu.get_barrier_semaphore()
    for j in range(1, count):
        peer = lax.rem(me + j, count)
        pl.semaphore_signal(
            barrier, inc=1, device_id=device(lax.div(peer, sub), lax.rem(peer, sub)), device_id_type=MESH
        )

    base = me * tile_count * 2
    tile_rows = [pairs[base + 2 * t] - r * sub for t in range(tile_count)]
    tile_cols = [pairs[base + 2 * t + 1] - r * sub for t in range(tile_count)]
    weights = []
    for n, m in own_slots:
        weights.append([flag((a == n) & (b == m)) for a, b in zip(tile_rows, tile_cols)])
    for n in range(sub):
        for off in range(1, SPAN):
            weights.append([
                flag((a == n) & (b >= off * sub) & (b < (off + 1) * sub))
                for a, b in zip(tile_rows, tile_cols)
            ])

    def named(off, column, block):
        peer = jnp.maximum((r - off) * sub + column, 0) * tile_count * 2
        hit = pairs[peer + 1] == block
        for t in range(1, tile_count):
            hit = hit | (pairs[peer + 2 * t + 1] == block)
        return flag(hit & (r >= off))

    wanted = [[named(off, s, r * sub + n) for n in range(sub)] for off in range(1, SPAN)]
    reads = []
    for off in range(1, SPAN):
        flags = []
        for m in range(sub):
            hit = tile_cols[0] == off * sub + m
            for t in range(1, tile_count):
                hit = hit | (tile_cols[t] == off * sub + m)
            flags.append(flag(hit))
        reads.append(flags)
    owned = [[named(off, column, me) for column in range(sub)] for off in range(1, SPAN)]

    chunk = 32

    @pl.loop(0, order // chunk)
    def _(i):
        span = pl.ds(pl.multiple_of(i * chunk, chunk), chunk)
        parts = [tiles[t, span, :].astype(jnp.float32) for t in range(tile_count)]
        for k, weight in enumerate(weights):
            total = weight[0] * parts[0]
            for t in range(1, tile_count):
                total = total + weight[t] * parts[t]
            slots[k, span, :] = total.astype(jnp.bfloat16)

    pl.semaphore_wait(barrier, count - 1)

    started = []

    def send(src, dst, send_sem, recv_sem, target, when=None):
        copy = pltpu.make_async_remote_copy(
            src_ref=src, dst_ref=dst, send_sem=send_sem, recv_sem=recv_sem,
            device_id=target, device_id_type=MESH,
        )
        started.append((copy, when))
        if when is None:
            copy.start()
        else:
            pl.when(when)(copy.start)
        return copy

    def arrive(copy, when=None):
        if when is None:
            copy.wait_recv()
        else:
            pl.when(when)(copy.wait_recv)

    ones = jnp.ones((16, order), jnp.bfloat16)
    for off in range(1, SPAN):
        for n in range(sub):
            deg_z[off - 1, n:n + 1, :] = plain(ones, slots[far_slot(n, off)])[:1]
    far_copies = {}
    for off in range(1, SPAN):
        for j in range(sub):
            target = device(jnp.minimum(r + off, rows - 1), lax.rem(s + j, sub))
            far_copies[off, j] = send(
                deg_z.at[off - 1], deg_z_in.at[off - 1, j],
                dz_s.at[off - 1, j], dz_r.at[off - 1, j], target, r + off < rows,
            )
    for n in range(sub):
        for m in range(sub):
            value = None
            if n <= m:
                value = turned(ones, slots[slot_of[(n, m)]])
            if m <= n:
                term = plain(ones, slots[slot_of[(m, n)]])
                value = term if value is None else value + term
            deg_x[n, m:m + 1, :] = value[:1]
        for off in range(1, SPAN):
            value = turned(ones, slots[far_slot(n, off)])[:1]
            for m in range(sub):
                k = off * sub + m
                deg_x[n, k:k + 1, :] = reads[off - 1][m] * value
    near_copies = []
    for j in range(1, sub):
        target = lax.rem(s + j, sub)
        near_copies.append(send(
            deg_x.at[target], deg_x_in.at[j - 1], dx_s.at[j - 1], dx_r.at[j - 1], device(r, target)
        ))
    total = deg_x[s]
    for j, copy in enumerate(near_copies):
        arrive(copy)
        total = total + deg_x_in[j]
    near_rows = total.shape[0]
    row_sums[...] = jnp.zeros_like(row_sums)
    row_sums[0:near_rows, :] = total
    for off in range(1, SPAN):
        first = near_rows + 8 * (off - 1)
        for j in range(sub):
            column = lax.rem(s - j + sub, sub)
            weight = owned[off - 1][0]
            for c in range(1, sub):
                weight = jnp.where(column == c, owned[off - 1][c], weight)
            arrive(far_copies[off, j], r >= off)
            row_sums[first:first + 8, :] = row_sums[first:first + 8, :] + weight * deg_z_in[off - 1, j]
    degree = jnp.sum(row_sums[...], axis=0, keepdims=True)
    root = 1.0 / jnp.sqrt(degree)

    def place_of(block):
        return lax.rem(s - block + sub, sub)

    def mean_row(distance, m):
        if distance >= 0:
            return distance * sub + m
        return near_rows + 8 * (-distance - 1) + m

    part = columns // CHUNKS
    spans = [slice(k * part, (k + 1) * part) for k in range(CHUNKS)]
    spread = (columns, 128)
    line = lax.broadcasted_iota(jnp.int32, (128, columns), 0)

    fields[0] = queries[...]
    for it in range(ITERS):
        scaled = root * fields[it]
        mean = jnp.mean(scaled, axis=1, keepdims=True).astype(jnp.bfloat16).astype(jnp.float32)
        panel[it, 0] = (scaled - mean).astype(jnp.bfloat16)
        gathers = {}
        for ch, span in enumerate(spans):
            for j in range(1, sub):
                gathers[ch, j] = send(
                    panel.at[it, 0, span], panel.at[it, j, span], panel_s.at[it, ch, j - 1],
                    panel_r.at[it, ch, j - 1], device(r, lax.rem(s + j, sub)),
                )
        means[it, FAR * sub] = jnp.broadcast_to(mean, spread).T[:16].astype(jnp.bfloat16)
        mean_copies = {}
        for d in range(-FAR, SPAN):
            for j in range(sub):
                k = (d + FAR) * sub + j
                if d == 0 and j == 0:
                    continue
                target = device(jnp.clip(r + d, 0, rows - 1), lax.rem(s + j, sub))
                mean_copies[d, j] = send(
                    means.at[it, FAR * sub], means.at[it, k], mean_s.at[it, k], mean_r.at[it, k],
                    target, None if d == 0 else (r + d >= 0) & (r + d < rows),
                )
        pays, backs = {}, {}
        for ch, span in enumerate(spans):
            for j in range(1, sub):
                arrive(gathers[ch, j])
            pieces = [panel[it, place_of(n), span] for n in range(sub)]
            for off in range(1, SPAN):
                total = wanted[off - 1][0] * pieces[0].astype(jnp.float32)
                for n in range(1, sub):
                    total = total + wanted[off - 1][n] * pieces[n].astype(jnp.float32)
                payload[it, off - 1, span] = total.astype(jnp.bfloat16)
                pays[ch, off] = send(
                    payload.at[it, off - 1, span], fetched.at[it, off - 1, span],
                    pay_s.at[it, ch, off - 1], pay_r.at[it, ch, off - 1],
                    device(jnp.maximum(r - off, 0), s), r >= off,
                )
            for off in range(1, SPAN):
                total = plain(pieces[0], slots[far_slot(0, off)])
                for n in range(1, sub):
                    total = total + plain(pieces[n], slots[far_slot(n, off)])
                back_out[it, off - 1, span] = total.astype(jnp.bfloat16)
                backs[ch, off] = send(
                    back_out.at[it, off - 1, span], back_in.at[it, off - 1, span],
                    back_s.at[it, ch, off - 1], back_r.at[it, ch, off - 1],
                    device(jnp.minimum(r + off, rows - 1), s), r + off < rows,
                )
        for n in range(sub):
            total = None
            for m in range(sub):
                source = panel[it, place_of(m)]
                if n <= m:
                    term = turned(source, slots[slot_of[(n, m)]])
                    total = term if total is None else total + term
                if m <= n:
                    term = plain(source, slots[slot_of[(m, n)]])
                    total = term if total is None else total + term
            acc[n] = total

        def finish(n, span):
            total = acc[n, span]
            for off in range(1, SPAN):
                weight = wanted[off - 1][0]
                for c in range(1, sub):
                    weight = jnp.where(n == c, wanted[off - 1][c], weight)
                total = total + weight * back_in[it, off - 1, span].astype(jnp.float32)
                total = total + turned(
                    fetched[it, off - 1, span], slots[far_slot(n, off)]
                )
            return total

        crossed = {}
        for ch, span in enumerate(spans):
            for off in range(1, SPAN):
                arrive(pays[ch, off], r + off < rows)
                arrive(backs[ch, off], r >= off)
            for j in range(1, sub):
                peer = lax.rem(s + j, sub)
                x_out[it, j - 1, span] = finish(peer, span).astype(jnp.bfloat16)
                crossed[ch, j] = send(
                    x_out.at[it, j - 1, span], x_in.at[it, j - 1, span], x_s.at[it, ch, j - 1],
                    x_r.at[it, ch, j - 1], device(r, peer),
                )
        for (d, j), copy in mean_copies.items():
            arrive(copy, None if d == 0 else (r - d >= 0) & (r - d < rows))
        table = jnp.zeros((128, columns), jnp.float32)
        for distance in range(-FAR, SPAN):
            for m in range(sub):
                row = means[it, (FAR - distance) * sub + place_of(m)].astype(jnp.float32)[:1]
                table = jnp.where(line == mean_row(distance, m), row, table)
        smooth = jnp.dot(
            table.T, row_sums[...], precision=lax.Precision.HIGHEST,
            preferred_element_type=jnp.float32,
        )
        for ch, span in enumerate(spans):
            total = smooth[span] + finish(s, span)
            for j in range(1, sub):
                arrive(crossed[ch, j])
                total = total + x_in[it, j - 1, span].astype(jnp.float32)
            fields[it + 1, span] = root * total

    lane = lax.broadcasted_iota(jnp.int32, (columns, 128), 1)
    table = jnp.zeros((columns, 128), jnp.float32)
    for k, (i, j) in enumerate(PAIRS):
        table = jnp.where(lane == k, jnp.sum(fields[i] * fields[j], axis=1, keepdims=True), table)
    gram_all[0] = table.T[:16]
    gram_copies = []
    for j in range(1, count):
        peer = lax.rem(me + j, count)
        gram_copies.append(send(
            gram_all.at[0], gram_all.at[j], gram_s.at[j - 1], gram_r.at[j - 1],
            device(lax.div(peer, sub), lax.rem(peer, sub)),
        ))
    total = gram_all[0]
    for j, copy in enumerate(gram_copies, 1):
        arrive(copy)
        total = total + gram_all[j]
    gram = {pair: total[k:k + 1] for k, pair in enumerate(PAIRS)}
    found, residual = step_coefficients(gram)
    rows_of = [c for c in found if c is not None] + residual
    table = jnp.zeros((128, columns), jnp.float32)
    for k, row in enumerate(rows_of):
        table = jnp.where(line == k, row, table)
    table = table.T
    total = table[:, 0:1] * fields[0]
    for k in range(1, ITERS):
        total = total + table[:, k:k + 1] * fields[k]
    found_out[...] = total
    total = table[:, ITERS:ITERS + 1] * fields[0]
    for k in range(1, BASIS):
        total = total + table[:, ITERS + k:ITERS + k + 1] * fields[k]
    residual_out[...] = total
    for copy, when in started:
        if when is None:
            copy.wait_send()
        else:
            pl.when(when)(copy.wait_send)


def local(queries, tiles, pair_blocks):
    rows = lax.axis_size("rows")
    sub = lax.axis_size("sub")
    count = rows * sub
    columns, order = queries.shape
    slot_count = sub * (sub + 1) // 2 + sub * FAR
    near_rows = -(-SPAN * sub // 8) * 8
    wide = lambda *shape: pltpu.VMEM(shape, jnp.float32)
    narrow = lambda *shape: pltpu.VMEM(shape, jnp.bfloat16)
    dma = lambda *shape: pltpu.SemaphoreType.DMA(shape)
    both = lambda *shape: [dma(*shape), dma(*shape)]
    vmem = pl.BlockSpec(memory_space=pltpu.VMEM)
    out = jax.ShapeDtypeStruct((columns, order), jnp.float32)
    return pl.pallas_call(
        functools.partial(kernel, rows, sub),
        out_shape=(out, out),
        in_specs=[pl.BlockSpec(memory_space=pltpu.SMEM), vmem, vmem],
        out_specs=(vmem, vmem),
        scratch_shapes=[
            narrow(slot_count, order, order),
            narrow(ITERS, sub, columns, order),
            narrow(ITERS, FAR, columns, order),
            narrow(ITERS, FAR, columns, order),
            narrow(ITERS, FAR, columns, order),
            narrow(ITERS, FAR, columns, order),
            wide(sub, columns, order),
            narrow(ITERS, sub - 1, columns, order),
            narrow(ITERS, sub - 1, columns, order),
            narrow(ITERS, (FAR + SPAN) * sub, 16, columns),
            wide(BASIS, columns, order),
            wide(FAR, 8, order),
            wide(FAR, sub, 8, order),
            wide(sub, near_rows, order),
            wide(sub - 1, near_rows, order),
            wide(128, order),
            wide(count, 16, columns),
            *both(ITERS, CHUNKS, sub - 1),
            *both(ITERS, CHUNKS, FAR),
            *both(ITERS, CHUNKS, FAR),
            *both(ITERS, CHUNKS, sub - 1),
            *both(ITERS, (FAR + SPAN) * sub),
            *both(FAR, sub),
            *both(sub - 1),
            *both(count - 1),
        ],
        compiler_params=pltpu.CompilerParams(
            collective_id=0, has_side_effects=True, vmem_limit_bytes=48 * 1024 * 1024
        ),
    )(pair_blocks.reshape(-1), queries, tiles)


def solution(mesh):
    return jax.shard_map(
        local,
        mesh=mesh,
        in_specs=(
            P("rep", ("groups", "rows", "sub")),
            P(("groups", "rows", "sub"), None, None),
            P("groups", None),
        ),
        out_specs=(P("rep", ("groups", "rows", "sub")), P("rep", ("groups", "rows", "sub"))),
        check_vma=False,
    )
```

```python
import functools

import jax
import jax.numpy as jnp
from jax import lax
from jax.experimental import pallas as pl
from jax.experimental.pallas import tpu as pltpu
from jax.sharding import PartitionSpec as P

SPAN = 3
ITERS = 3
DAMPING = 0.9
FAR = SPAN - 1
BASIS = ITERS + 1
CHUNKS = 4
GROUPS = 4
MESH = pl.DeviceIdType.MESH
PAIRS = [(i, j) for i in range(BASIS) for j in range(i, BASIS)]


def plain(left, right):
    return jnp.dot(left, right, preferred_element_type=jnp.float32)


def turned(left, right):
    return lax.dot_general(
        left, right, (((1,), (1,)), ((), ())), preferred_element_type=jnp.float32
    )


def flag(condition):
    return jnp.where(condition, 1.0, 0.0).astype(jnp.float32)


def step_coefficients(gram):
    def inner(first, second):
        total = None
        for i in range(BASIS):
            for j in range(BASIS):
                if first[i] is None or second[j] is None:
                    continue
                term = first[i] * second[j] * gram[(min(i, j), max(i, j))]
                total = term if total is None else total + term
        return total

    def plus(first, factor, second):
        out = []
        for a, b in zip(first, second):
            if b is None:
                out.append(a)
            elif a is None:
                out.append(factor * b)
            else:
                out.append(a + factor * b)
        return out

    def mapped_of(vector):
        out = []
        for k in range(BASIS):
            low = vector[k - 1] if k else None
            if low is None:
                out.append(vector[k])
            elif vector[k] is None:
                out.append(-DAMPING * low)
            else:
                out.append(vector[k] - DAMPING * low)
        return out

    one = jnp.ones_like(gram[(0, 0)])
    found = [None] * BASIS
    residual = [one] + [None] * ITERS
    direction = list(residual)
    norm_now = gram[(0, 0)]
    for _ in range(ITERS):
        mapped = mapped_of(direction)
        step = norm_now / inner(direction, mapped)
        found = plus(found, step, direction)
        residual = plus(residual, -step, mapped)
        norm_next = inner(residual, residual)
        direction = plus(residual, norm_next / norm_now, direction)
        norm_now = norm_next
    return found, residual


def kernel(
    rows, sub, pairs, queries, tiles_far, found_out, residual_out,
    tiles, load_s, slots, panel, payload, fetched, back_out, back_in, acc, x_out, x_in, means, fields,
    deg_z, deg_z_in, deg_x, deg_x_in, row_sums, gram_all,
    panel_s, panel_r, pay_s, pay_r, back_s, back_r, x_s, x_r, mean_s, mean_r,
    dz_s, dz_r, dx_s, dx_r, gram_s, gram_r,
):
    r = lax.axis_index("rows")
    s = lax.axis_index("sub")
    count = rows * sub
    me = r * sub + s
    tile_count, order, _ = tiles.shape
    columns = queries.shape[0]
    own_slots = [(n, m) for n in range(sub) for m in range(n, sub)]
    slot_of = {pair: k for k, pair in enumerate(own_slots)}
    first_far = len(own_slots)

    def far_slot(n, off):
        return first_far + n * FAR + off - 1

    def device(row, column):
        return {"rows": row, "sub": column}

    group = order // GROUPS
    loads = []
    for g in range(GROUPS):
        span = pl.ds(g * group, group)
        loads.append(pltpu.make_async_copy(tiles_far.at[:, span], tiles.at[:, span], load_s.at[g]))
        loads[-1].start()

    for landing in (fetched, back_in, means, deg_z_in, deg_z, deg_x):
        landing[...] = jnp.zeros_like(landing)

    barrier = pltpu.get_barrier_semaphore()
    for j in range(1, count):
        peer = lax.rem(me + j, count)
        pl.semaphore_signal(
            barrier, inc=1, device_id=device(lax.div(peer, sub), lax.rem(peer, sub)), device_id_type=MESH
        )

    base = me * tile_count * 2
    tile_rows = [pairs[base + 2 * t] - r * sub for t in range(tile_count)]
    tile_cols = [pairs[base + 2 * t + 1] - r * sub for t in range(tile_count)]
    weights = []
    for n, m in own_slots:
        weights.append([flag((a == n) & (b == m)) for a, b in zip(tile_rows, tile_cols)])
    for n in range(sub):
        for off in range(1, SPAN):
            weights.append([
                flag((a == n) & (b >= off * sub) & (b < (off + 1) * sub))
                for a, b in zip(tile_rows, tile_cols)
            ])

    def named(off, column, block):
        peer = jnp.maximum((r - off) * sub + column, 0) * tile_count * 2
        hit = pairs[peer + 1] == block
        for t in range(1, tile_count):
            hit = hit | (pairs[peer + 2 * t + 1] == block)
        return flag(hit & (r >= off))

    wanted = [[named(off, s, r * sub + n) for n in range(sub)] for off in range(1, SPAN)]
    reads = []
    for off in range(1, SPAN):
        flags = []
        for m in range(sub):
            hit = tile_cols[0] == off * sub + m
            for t in range(1, tile_count):
                hit = hit | (tile_cols[t] == off * sub + m)
            flags.append(flag(hit))
        reads.append(flags)
    owned = [[named(off, column, me) for column in range(sub)] for off in range(1, SPAN)]

    chunk = 32

    def sum_tiles(i):
        span = pl.ds(pl.multiple_of(i * chunk, chunk), chunk)
        parts = [tiles[t, span, :].astype(jnp.float32) for t in range(tile_count)]
        for k, weight in enumerate(weights):
            total = weight[0] * parts[0]
            for t in range(1, tile_count):
                total = total + weight[t] * parts[t]
            slots[k, span, :] = total.astype(jnp.bfloat16)

    for g in range(GROUPS):
        loads[g].wait()
        pl.loop(g * group // chunk, (g + 1) * group // chunk)(sum_tiles)

    pl.semaphore_wait(barrier, count - 1)

    started = []

    def send(src, dst, send_sem, recv_sem, target, when=None):
        copy = pltpu.make_async_remote_copy(
            src_ref=src, dst_ref=dst, send_sem=send_sem, recv_sem=recv_sem,
            device_id=target, device_id_type=MESH,
        )
        started.append((copy, when))
        if when is None:
            copy.start()
        else:
            pl.when(when)(copy.start)
        return copy

    def arrive(copy, when=None):
        if when is None:
            copy.wait_recv()
        else:
            pl.when(when)(copy.wait_recv)

    ones = jnp.ones((16, order), jnp.bfloat16)
    for off in range(1, SPAN):
        for n in range(sub):
            deg_z[off - 1, n:n + 1, :] = plain(ones, slots[far_slot(n, off)])[:1]
    far_copies = {}
    for off in range(1, SPAN):
        for j in range(sub):
            target = device(jnp.minimum(r + off, rows - 1), lax.rem(s + j, sub))
            far_copies[off, j] = send(
                deg_z.at[off - 1], deg_z_in.at[off - 1, j],
                dz_s.at[off - 1, j], dz_r.at[off - 1, j], target, r + off < rows,
            )
    for n in range(sub):
        for m in range(sub):
            value = None
            if n <= m:
                value = turned(ones, slots[slot_of[(n, m)]])
            if m <= n:
                term = plain(ones, slots[slot_of[(m, n)]])
                value = term if value is None else value + term
            deg_x[n, m:m + 1, :] = value[:1]
        for off in range(1, SPAN):
            value = turned(ones, slots[far_slot(n, off)])[:1]
            for m in range(sub):
                k = off * sub + m
                deg_x[n, k:k + 1, :] = reads[off - 1][m] * value
    near_copies = []
    for j in range(1, sub):
        target = lax.rem(s + j, sub)
        near_copies.append(send(
            deg_x.at[target], deg_x_in.at[j - 1], dx_s.at[j - 1], dx_r.at[j - 1], device(r, target)
        ))
    total = deg_x[s]
    for j, copy in enumerate(near_copies):
        arrive(copy)
        total = total + deg_x_in[j]
    near_rows = total.shape[0]
    row_sums[...] = jnp.zeros_like(row_sums)
    row_sums[0:near_rows, :] = total
    for off in range(1, SPAN):
        first = near_rows + 8 * (off - 1)
        for j in range(sub):
            column = lax.rem(s - j + sub, sub)
            weight = owned[off - 1][0]
            for c in range(1, sub):
                weight = jnp.where(column == c, owned[off - 1][c], weight)
            arrive(far_copies[off, j], r >= off)
            row_sums[first:first + 8, :] = row_sums[first:first + 8, :] + weight * deg_z_in[off - 1, j]
    degree = jnp.sum(row_sums[...], axis=0, keepdims=True)
    root = 1.0 / jnp.sqrt(degree)

    def place_of(block):
        return lax.rem(s - block + sub, sub)

    def mean_row(distance, m):
        if distance >= 0:
            return distance * sub + m
        return near_rows + 8 * (-distance - 1) + m

    part = columns // CHUNKS
    spans = [slice(k * part, (k + 1) * part) for k in range(CHUNKS)]
    spread = (columns, 128)
    line = lax.broadcasted_iota(jnp.int32, (128, columns), 0)

    fields[0] = queries[...]
    for it in range(ITERS):
        scaled = root * fields[it]
        mean = jnp.mean(scaled, axis=1, keepdims=True).astype(jnp.bfloat16).astype(jnp.float32)
        panel[it, 0] = (scaled - mean).astype(jnp.bfloat16)
        gathers = {}
        for ch, span in enumerate(spans):
            for j in range(1, sub):
                gathers[ch, j] = send(
                    panel.at[it, 0, span], panel.at[it, j, span], panel_s.at[it, ch, j - 1],
                    panel_r.at[it, ch, j - 1], device(r, lax.rem(s + j, sub)),
                )
        means[it, FAR * sub] = jnp.broadcast_to(mean, spread).T[:16].astype(jnp.bfloat16)
        mean_copies = {}
        for d in range(-FAR, SPAN):
            for j in range(sub):
                k = (d + FAR) * sub + j
                if d == 0 and j == 0:
                    continue
                target = device(jnp.clip(r + d, 0, rows - 1), lax.rem(s + j, sub))
                mean_copies[d, j] = send(
                    means.at[it, FAR * sub], means.at[it, k], mean_s.at[it, k], mean_r.at[it, k],
                    target, None if d == 0 else (r + d >= 0) & (r + d < rows),
                )
        pays, backs = {}, {}
        for ch, span in enumerate(spans):
            for j in range(1, sub):
                arrive(gathers[ch, j])
            pieces = [panel[it, place_of(n), span] for n in range(sub)]
            for off in range(FAR, 0, -1):
                total = wanted[off - 1][0] * pieces[0].astype(jnp.float32)
                for n in range(1, sub):
                    total = total + wanted[off - 1][n] * pieces[n].astype(jnp.float32)
                payload[it, off - 1, span] = total.astype(jnp.bfloat16)
                pays[ch, off] = send(
                    payload.at[it, off - 1, span], fetched.at[it, off - 1, span],
                    pay_s.at[it, ch, off - 1], pay_r.at[it, ch, off - 1],
                    device(jnp.maximum(r - off, 0), s), r >= off,
                )
            for off in range(FAR, 0, -1):
                total = plain(pieces[0], slots[far_slot(0, off)])
                for n in range(1, sub):
                    total = total + plain(pieces[n], slots[far_slot(n, off)])
                back_out[it, off - 1, span] = total.astype(jnp.bfloat16)
                backs[ch, off] = send(
                    back_out.at[it, off - 1, span], back_in.at[it, off - 1, span],
                    back_s.at[it, ch, off - 1], back_r.at[it, ch, off - 1],
                    device(jnp.minimum(r + off, rows - 1), s), r + off < rows,
                )
        for n in range(sub):
            total = None
            for m in range(sub):
                source = panel[it, place_of(m)]
                if n <= m:
                    term = turned(source, slots[slot_of[(n, m)]])
                    total = term if total is None else total + term
                if m <= n:
                    term = plain(source, slots[slot_of[(m, n)]])
                    total = term if total is None else total + term
            acc[n] = total

        def finish(n, span):
            total = acc[n, span]
            for off in range(1, SPAN):
                weight = wanted[off - 1][0]
                for c in range(1, sub):
                    weight = jnp.where(n == c, wanted[off - 1][c], weight)
                total = total + weight * back_in[it, off - 1, span].astype(jnp.float32)
                total = total + turned(
                    fetched[it, off - 1, span], slots[far_slot(n, off)]
                )
            return total

        crossed = {}
        for ch, span in enumerate(spans):
            for off in range(1, SPAN):
                arrive(pays[ch, off], r + off < rows)
                arrive(backs[ch, off], r >= off)
            for j in range(1, sub):
                peer = lax.rem(s + j, sub)
                x_out[it, j - 1, span] = finish(peer, span).astype(jnp.bfloat16)
                crossed[ch, j] = send(
                    x_out.at[it, j - 1, span], x_in.at[it, j - 1, span], x_s.at[it, ch, j - 1],
                    x_r.at[it, ch, j - 1], device(r, peer),
                )
        for (d, j), copy in mean_copies.items():
            arrive(copy, None if d == 0 else (r - d >= 0) & (r - d < rows))
        table = jnp.zeros((128, columns), jnp.float32)
        for distance in range(-FAR, SPAN):
            for m in range(sub):
                row = means[it, (FAR - distance) * sub + place_of(m)].astype(jnp.float32)[:1]
                table = jnp.where(line == mean_row(distance, m), row, table)
        smooth = jnp.dot(
            table.T, row_sums[...], precision=lax.Precision.HIGHEST,
            preferred_element_type=jnp.float32,
        )
        for ch, span in enumerate(spans):
            total = smooth[span] + finish(s, span)
            for j in range(1, sub):
                arrive(crossed[ch, j])
                total = total + x_in[it, j - 1, span].astype(jnp.float32)
            fields[it + 1, span] = root * total

    lane = lax.broadcasted_iota(jnp.int32, (columns, 128), 1)
    table = jnp.zeros((columns, 128), jnp.float32)
    for k, (i, j) in enumerate(PAIRS):
        table = jnp.where(lane == k, jnp.sum(fields[i] * fields[j], axis=1, keepdims=True), table)
    gram_all[0] = table.T[:16]
    gram_copies = []
    for j in range(1, count):
        peer = lax.rem(me + j, count)
        gram_copies.append(send(
            gram_all.at[0], gram_all.at[j], gram_s.at[j - 1], gram_r.at[j - 1],
            device(lax.div(peer, sub), lax.rem(peer, sub)),
        ))
    total = gram_all[0]
    for j, copy in enumerate(gram_copies, 1):
        arrive(copy)
        total = total + gram_all[j]
    gram = {pair: total[k:k + 1] for k, pair in enumerate(PAIRS)}
    found, residual = step_coefficients(gram)
    rows_of = [c for c in found if c is not None] + residual
    table = jnp.zeros((128, columns), jnp.float32)
    for k, row in enumerate(rows_of):
        table = jnp.where(line == k, row, table)
    table = table.T
    total = table[:, 0:1] * fields[0]
    for k in range(1, ITERS):
        total = total + table[:, k:k + 1] * fields[k]
    found_out[...] = total
    total = table[:, ITERS:ITERS + 1] * fields[0]
    for k in range(1, BASIS):
        total = total + table[:, ITERS + k:ITERS + k + 1] * fields[k]
    residual_out[...] = total
    for copy, when in started:
        if when is None:
            copy.wait_send()
        else:
            pl.when(when)(copy.wait_send)


def local(queries, tiles, pair_blocks):
    rows = lax.axis_size("rows")
    sub = lax.axis_size("sub")
    count = rows * sub
    columns, order = queries.shape
    slot_count = sub * (sub + 1) // 2 + sub * FAR
    near_rows = -(-SPAN * sub // 8) * 8
    wide = lambda *shape: pltpu.VMEM(shape, jnp.float32)
    narrow = lambda *shape: pltpu.VMEM(shape, jnp.bfloat16)
    dma = lambda *shape: pltpu.SemaphoreType.DMA(shape)
    both = lambda *shape: [dma(*shape), dma(*shape)]
    vmem = pl.BlockSpec(memory_space=pltpu.VMEM)
    out = jax.ShapeDtypeStruct((columns, order), jnp.float32)
    return pl.pallas_call(
        functools.partial(kernel, rows, sub),
        out_shape=(out, out),
        in_specs=[pl.BlockSpec(memory_space=pltpu.SMEM), vmem, pl.BlockSpec(memory_space=pl.ANY)],
        out_specs=(vmem, vmem),
        scratch_shapes=[
            narrow(*tiles.shape),
            dma(GROUPS),
            narrow(slot_count, order, order),
            narrow(ITERS, sub, columns, order),
            narrow(ITERS, FAR, columns, order),
            narrow(ITERS, FAR, columns, order),
            narrow(ITERS, FAR, columns, order),
            narrow(ITERS, FAR, columns, order),
            wide(sub, columns, order),
            narrow(ITERS, sub - 1, columns, order),
            narrow(ITERS, sub - 1, columns, order),
            narrow(ITERS, (FAR + SPAN) * sub, 16, columns),
            wide(BASIS, columns, order),
            wide(FAR, 8, order),
            wide(FAR, sub, 8, order),
            wide(sub, near_rows, order),
            wide(sub - 1, near_rows, order),
            wide(128, order),
            wide(count, 16, columns),
            *both(ITERS, CHUNKS, sub - 1),
            *both(ITERS, CHUNKS, FAR),
            *both(ITERS, CHUNKS, FAR),
            *both(ITERS, CHUNKS, sub - 1),
            *both(ITERS, (FAR + SPAN) * sub),
            *both(FAR, sub),
            *both(sub - 1),
            *both(count - 1),
        ],
        compiler_params=pltpu.CompilerParams(
            collective_id=0, has_side_effects=True, vmem_limit_bytes=48 * 1024 * 1024
        ),
    )(pair_blocks.reshape(-1), queries, tiles)


def solution(mesh):
    return jax.shard_map(
        local,
        mesh=mesh,
        in_specs=(
            P("rep", ("groups", "rows", "sub")),
            P(("groups", "rows", "sub"), None, None),
            P("groups", None),
        ),
        out_specs=(P("rep", ("groups", "rows", "sub")), P("rep", ("groups", "rows", "sub"))),
        check_vma=False,
    )
```

```python
import functools

import jax
import jax.numpy as jnp
from jax import lax
from jax.experimental import pallas as pl
from jax.experimental.pallas import tpu as pltpu
from jax.sharding import PartitionSpec as P

SPAN = 3
ITERS = 3
DAMPING = 0.9
FAR = SPAN - 1
BASIS = ITERS + 1
CHUNKS = 4
GROUPS = 4
MESH = pl.DeviceIdType.MESH
PAIRS = [(i, j) for i in range(BASIS) for j in range(i, BASIS)]


def plain(left, right):
    return jnp.dot(left, right, preferred_element_type=jnp.float32)


def turned(left, right):
    return lax.dot_general(
        left, right, (((1,), (1,)), ((), ())), preferred_element_type=jnp.float32
    )


def flag(condition):
    return jnp.where(condition, 1.0, 0.0).astype(jnp.float32)


def step_coefficients(gram):
    def inner(first, second):
        total = None
        for i in range(BASIS):
            for j in range(BASIS):
                if first[i] is None or second[j] is None:
                    continue
                term = first[i] * second[j] * gram[(min(i, j), max(i, j))]
                total = term if total is None else total + term
        return total

    def plus(first, factor, second):
        out = []
        for a, b in zip(first, second):
            if b is None:
                out.append(a)
            elif a is None:
                out.append(factor * b)
            else:
                out.append(a + factor * b)
        return out

    def mapped_of(vector):
        out = []
        for k in range(BASIS):
            low = vector[k - 1] if k else None
            if low is None:
                out.append(vector[k])
            elif vector[k] is None:
                out.append(-DAMPING * low)
            else:
                out.append(vector[k] - DAMPING * low)
        return out

    one = jnp.ones_like(gram[(0, 0)])
    found = [None] * BASIS
    residual = [one] + [None] * ITERS
    direction = list(residual)
    norm_now = gram[(0, 0)]
    for _ in range(ITERS):
        mapped = mapped_of(direction)
        step = norm_now / inner(direction, mapped)
        found = plus(found, step, direction)
        residual = plus(residual, -step, mapped)
        norm_next = inner(residual, residual)
        direction = plus(residual, norm_next / norm_now, direction)
        norm_now = norm_next
    return found, residual


def kernel(
    rows, sub, pairs, queries, tiles_far, found_out, residual_out,
    tiles, load_s, slots, panel, payload, fetched, back_out, back_in, acc, x_out, x_in, means, fields,
    deg_z, deg_z_in, deg_x, deg_x_in, row_sums, gram_all,
    panel_s, panel_r, pay_s, pay_r, back_s, back_r, x_s, x_r, mean_s, mean_r,
    dz_s, dz_r, dx_s, dx_r, gram_s, gram_r,
):
    r = lax.axis_index("rows")
    s = lax.axis_index("sub")
    count = rows * sub
    me = r * sub + s
    tile_count, order, _ = tiles.shape
    columns = queries.shape[0]
    own_slots = [(n, m) for n in range(sub) for m in range(n, sub)]
    slot_of = {pair: k for k, pair in enumerate(own_slots)}
    first_far = len(own_slots)

    def far_slot(n, off):
        return first_far + n * FAR + off - 1

    def device(row, column):
        return {"rows": row, "sub": column}

    group = order // GROUPS
    loads = []
    for g in range(GROUPS):
        span = pl.ds(g * group, group)
        loads.append(pltpu.make_async_copy(tiles_far.at[:, span], tiles.at[:, span], load_s.at[g]))
        loads[-1].start()

    for landing in (fetched, back_in, means, deg_z_in, deg_z, deg_x):
        landing[...] = jnp.zeros_like(landing)

    barrier = pltpu.get_barrier_semaphore()
    for j in range(1, count):
        peer = lax.rem(me + j, count)
        pl.semaphore_signal(
            barrier, inc=1, device_id=device(lax.div(peer, sub), lax.rem(peer, sub)), device_id_type=MESH
        )

    base = me * tile_count * 2
    tile_rows = [pairs[base + 2 * t] - r * sub for t in range(tile_count)]
    tile_cols = [pairs[base + 2 * t + 1] - r * sub for t in range(tile_count)]
    weights = []
    for n, m in own_slots:
        weights.append([flag((a == n) & (b == m)) for a, b in zip(tile_rows, tile_cols)])
    for n in range(sub):
        for off in range(1, SPAN):
            weights.append([
                flag((a == n) & (b >= off * sub) & (b < (off + 1) * sub))
                for a, b in zip(tile_rows, tile_cols)
            ])

    def named(off, column, block):
        peer = jnp.maximum((r - off) * sub + column, 0) * tile_count * 2
        hit = pairs[peer + 1] == block
        for t in range(1, tile_count):
            hit = hit | (pairs[peer + 2 * t + 1] == block)
        return flag(hit & (r >= off))

    wanted = [[named(off, s, r * sub + n) for n in range(sub)] for off in range(1, SPAN)]
    reads = []
    for off in range(1, SPAN):
        flags = []
        for m in range(sub):
            hit = tile_cols[0] == off * sub + m
            for t in range(1, tile_count):
                hit = hit | (tile_cols[t] == off * sub + m)
            flags.append(flag(hit))
        reads.append(flags)
    owned = [[named(off, column, me) for column in range(sub)] for off in range(1, SPAN)]

    chunk = 32

    def sum_tiles(i):
        span = pl.ds(pl.multiple_of(i * chunk, chunk), chunk)
        parts = [tiles[t, span, :].astype(jnp.float32) for t in range(tile_count)]
        for k, weight in enumerate(weights):
            total = weight[0] * parts[0]
            for t in range(1, tile_count):
                total = total + weight[t] * parts[t]
            slots[k, span, :] = total.astype(jnp.bfloat16)

    for g in range(GROUPS):
        loads[g].wait()
        pl.loop(g * group // chunk, (g + 1) * group // chunk)(sum_tiles)

    pl.semaphore_wait(barrier, count - 1)

    started = []

    def send(src, dst, send_sem, recv_sem, target, when=None):
        copy = pltpu.make_async_remote_copy(
            src_ref=src, dst_ref=dst, send_sem=send_sem, recv_sem=recv_sem,
            device_id=target, device_id_type=MESH,
        )
        started.append((copy, when))
        if when is None:
            copy.start()
        else:
            pl.when(when)(copy.start)
        return copy

    def arrive(copy, when=None):
        if when is None:
            copy.wait_recv()
        else:
            pl.when(when)(copy.wait_recv)

    ones = jnp.ones((16, order), jnp.bfloat16)
    for off in range(1, SPAN):
        for n in range(sub):
            deg_z[off - 1, n:n + 1, :] = plain(ones, slots[far_slot(n, off)])[:1]
    far_copies = {}
    for off in range(1, SPAN):
        for j in range(sub):
            target = device(jnp.minimum(r + off, rows - 1), lax.rem(s + j, sub))
            far_copies[off, j] = send(
                deg_z.at[off - 1], deg_z_in.at[off - 1, j],
                dz_s.at[off - 1, j], dz_r.at[off - 1, j], target, r + off < rows,
            )
    for n in range(sub):
        for m in range(sub):
            value = None
            if n <= m:
                value = turned(ones, slots[slot_of[(n, m)]])
            if m <= n:
                term = plain(ones, slots[slot_of[(m, n)]])
                value = term if value is None else value + term
            deg_x[n, m:m + 1, :] = value[:1]
        for off in range(1, SPAN):
            value = turned(ones, slots[far_slot(n, off)])[:1]
            for m in range(sub):
                k = off * sub + m
                deg_x[n, k:k + 1, :] = reads[off - 1][m] * value
    near_copies = []
    for j in range(1, sub):
        target = lax.rem(s + j, sub)
        near_copies.append(send(
            deg_x.at[target], deg_x_in.at[j - 1], dx_s.at[j - 1], dx_r.at[j - 1], device(r, target)
        ))
    total = deg_x[s]
    for j, copy in enumerate(near_copies):
        arrive(copy)
        total = total + deg_x_in[j]
    near_rows = total.shape[0]
    row_sums[...] = jnp.zeros_like(row_sums)
    row_sums[0:near_rows, :] = total
    for off in range(1, SPAN):
        first = near_rows + 8 * (off - 1)
        for j in range(sub):
            column = lax.rem(s - j + sub, sub)
            weight = owned[off - 1][0]
            for c in range(1, sub):
                weight = jnp.where(column == c, owned[off - 1][c], weight)
            arrive(far_copies[off, j], r >= off)
            row_sums[first:first + 8, :] = row_sums[first:first + 8, :] + weight * deg_z_in[off - 1, j]
    degree = jnp.sum(row_sums[...], axis=0, keepdims=True)
    root = 1.0 / jnp.sqrt(degree)

    def place_of(block):
        return lax.rem(s - block + sub, sub)

    def mean_row(distance, m):
        if distance >= 0:
            return distance * sub + m
        return near_rows + 8 * (-distance - 1) + m

    part = columns // CHUNKS
    spans = [slice(k * part, (k + 1) * part) for k in range(CHUNKS)]
    spread = (columns, 128)
    line = lax.broadcasted_iota(jnp.int32, (128, columns), 0)

    fields[0] = queries[...]
    for it in range(ITERS):
        scaled = root * fields[it]
        mean = jnp.mean(scaled, axis=1, keepdims=True).astype(jnp.bfloat16).astype(jnp.float32)
        panel[it, 0] = (scaled - mean).astype(jnp.bfloat16)
        gathers = {}
        for ch, span in enumerate(spans):
            for j in range(1, sub):
                gathers[ch, j] = send(
                    panel.at[it, 0, span], panel.at[it, j, span], panel_s.at[it, ch, j - 1],
                    panel_r.at[it, ch, j - 1], device(r, lax.rem(s + j, sub)),
                )
        means[it, FAR * sub] = jnp.broadcast_to(mean, spread).T[:16].astype(jnp.bfloat16)
        pays, backs = {}, {}
        for ch, span in enumerate(spans):
            for j in range(1, sub):
                arrive(gathers[ch, j])
            pieces = [panel[it, place_of(n), span] for n in range(sub)]
            for off in range(1, SPAN):
                total = wanted[off - 1][0] * pieces[0].astype(jnp.float32)
                for n in range(1, sub):
                    total = total + wanted[off - 1][n] * pieces[n].astype(jnp.float32)
                payload[it, off - 1, span] = total.astype(jnp.bfloat16)
                pays[ch, off] = send(
                    payload.at[it, off - 1, span], fetched.at[it, off - 1, span],
                    pay_s.at[it, ch, off - 1], pay_r.at[it, ch, off - 1],
                    device(jnp.maximum(r - off, 0), s), r >= off,
                )
            for off in range(1, SPAN):
                total = plain(pieces[0], slots[far_slot(0, off)])
                for n in range(1, sub):
                    total = total + plain(pieces[n], slots[far_slot(n, off)])
                back_out[it, off - 1, span] = total.astype(jnp.bfloat16)
                backs[ch, off] = send(
                    back_out.at[it, off - 1, span], back_in.at[it, off - 1, span],
                    back_s.at[it, ch, off - 1], back_r.at[it, ch, off - 1],
                    device(jnp.minimum(r + off, rows - 1), s), r + off < rows,
                )
        mean_copies = {}
        for d in range(-FAR, SPAN):
            for j in range(sub):
                k = (d + FAR) * sub + j
                if d == 0 and j == 0:
                    continue
                target = device(jnp.clip(r + d, 0, rows - 1), lax.rem(s + j, sub))
                mean_copies[d, j] = send(
                    means.at[it, FAR * sub], means.at[it, k], mean_s.at[it, k], mean_r.at[it, k],
                    target, None if d == 0 else (r + d >= 0) & (r + d < rows),
                )
        for n in range(sub):
            total = None
            for m in range(sub):
                source = panel[it, place_of(m)]
                if n <= m:
                    term = turned(source, slots[slot_of[(n, m)]])
                    total = term if total is None else total + term
                if m <= n:
                    term = plain(source, slots[slot_of[(m, n)]])
                    total = term if total is None else total + term
            acc[n] = total

        def finish(n, span):
            total = acc[n, span]
            for off in range(1, SPAN):
                weight = wanted[off - 1][0]
                for c in range(1, sub):
                    weight = jnp.where(n == c, wanted[off - 1][c], weight)
                total = total + weight * back_in[it, off - 1, span].astype(jnp.float32)
                total = total + turned(
                    fetched[it, off - 1, span], slots[far_slot(n, off)]
                )
            return total

        crossed = {}
        for ch, span in enumerate(spans):
            for off in range(1, SPAN):
                arrive(pays[ch, off], r + off < rows)
                arrive(backs[ch, off], r >= off)
            for j in range(1, sub):
                peer = lax.rem(s + j, sub)
                x_out[it, j - 1, span] = finish(peer, span).astype(jnp.bfloat16)
                crossed[ch, j] = send(
                    x_out.at[it, j - 1, span], x_in.at[it, j - 1, span], x_s.at[it, ch, j - 1],
                    x_r.at[it, ch, j - 1], device(r, peer),
                )
        for (d, j), copy in mean_copies.items():
            arrive(copy, None if d == 0 else (r - d >= 0) & (r - d < rows))
        table = jnp.zeros((128, columns), jnp.float32)
        for distance in range(-FAR, SPAN):
            for m in range(sub):
                row = means[it, (FAR - distance) * sub + place_of(m)].astype(jnp.float32)[:1]
                table = jnp.where(line == mean_row(distance, m), row, table)
        smooth = jnp.dot(
            table.T, row_sums[...], precision=lax.Precision.HIGHEST,
            preferred_element_type=jnp.float32,
        )
        for ch, span in enumerate(spans):
            total = smooth[span] + finish(s, span)
            for j in range(1, sub):
                arrive(crossed[ch, j])
                total = total + x_in[it, j - 1, span].astype(jnp.float32)
            fields[it + 1, span] = root * total

    lane = lax.broadcasted_iota(jnp.int32, (columns, 128), 1)
    table = jnp.zeros((columns, 128), jnp.float32)
    for k, (i, j) in enumerate(PAIRS):
        table = jnp.where(lane == k, jnp.sum(fields[i] * fields[j], axis=1, keepdims=True), table)
    gram_all[0] = table.T[:16]
    gram_copies = []
    for j in range(1, count):
        peer = lax.rem(me + j, count)
        gram_copies.append(send(
            gram_all.at[0], gram_all.at[j], gram_s.at[j - 1], gram_r.at[j - 1],
            device(lax.div(peer, sub), lax.rem(peer, sub)),
        ))
    total = gram_all[0]
    for j, copy in enumerate(gram_copies, 1):
        arrive(copy)
        total = total + gram_all[j]
    gram = {pair: total[k:k + 1] for k, pair in enumerate(PAIRS)}
    found, residual = step_coefficients(gram)
    rows_of = [c for c in found if c is not None] + residual
    table = jnp.zeros((128, columns), jnp.float32)
    for k, row in enumerate(rows_of):
        table = jnp.where(line == k, row, table)
    table = table.T
    total = table[:, 0:1] * fields[0]
    for k in range(1, ITERS):
        total = total + table[:, k:k + 1] * fields[k]
    found_out[...] = total
    total = table[:, ITERS:ITERS + 1] * fields[0]
    for k in range(1, BASIS):
        total = total + table[:, ITERS + k:ITERS + k + 1] * fields[k]
    residual_out[...] = total
    for copy, when in started:
        if when is None:
            copy.wait_send()
        else:
            pl.when(when)(copy.wait_send)


def local(queries, tiles, pair_blocks):
    rows = lax.axis_size("rows")
    sub = lax.axis_size("sub")
    count = rows * sub
    columns, order = queries.shape
    slot_count = sub * (sub + 1) // 2 + sub * FAR
    near_rows = -(-SPAN * sub // 8) * 8
    wide = lambda *shape: pltpu.VMEM(shape, jnp.float32)
    narrow = lambda *shape: pltpu.VMEM(shape, jnp.bfloat16)
    dma = lambda *shape: pltpu.SemaphoreType.DMA(shape)
    both = lambda *shape: [dma(*shape), dma(*shape)]
    vmem = pl.BlockSpec(memory_space=pltpu.VMEM)
    out = jax.ShapeDtypeStruct((columns, order), jnp.float32)
    return pl.pallas_call(
        functools.partial(kernel, rows, sub),
        out_shape=(out, out),
        in_specs=[pl.BlockSpec(memory_space=pltpu.SMEM), vmem, pl.BlockSpec(memory_space=pl.ANY)],
        out_specs=(vmem, vmem),
        scratch_shapes=[
            narrow(*tiles.shape),
            dma(GROUPS),
            narrow(slot_count, order, order),
            narrow(ITERS, sub, columns, order),
            narrow(ITERS, FAR, columns, order),
            narrow(ITERS, FAR, columns, order),
            narrow(ITERS, FAR, columns, order),
            narrow(ITERS, FAR, columns, order),
            wide(sub, columns, order),
            narrow(ITERS, sub - 1, columns, order),
            narrow(ITERS, sub - 1, columns, order),
            narrow(ITERS, (FAR + SPAN) * sub, 16, columns),
            wide(BASIS, columns, order),
            wide(FAR, 8, order),
            wide(FAR, sub, 8, order),
            wide(sub, near_rows, order),
            wide(sub - 1, near_rows, order),
            wide(128, order),
            wide(count, 16, columns),
            *both(ITERS, CHUNKS, sub - 1),
            *both(ITERS, CHUNKS, FAR),
            *both(ITERS, CHUNKS, FAR),
            *both(ITERS, CHUNKS, sub - 1),
            *both(ITERS, (FAR + SPAN) * sub),
            *both(FAR, sub),
            *both(sub - 1),
            *both(count - 1),
        ],
        compiler_params=pltpu.CompilerParams(
            collective_id=0, has_side_effects=True, vmem_limit_bytes=48 * 1024 * 1024
        ),
    )(pair_blocks.reshape(-1), queries, tiles)


def solution(mesh):
    return jax.shard_map(
        local,
        mesh=mesh,
        in_specs=(
            P("rep", ("groups", "rows", "sub")),
            P(("groups", "rows", "sub"), None, None),
            P("groups", None),
        ),
        out_specs=(P("rep", ("groups", "rows", "sub")), P("rep", ("groups", "rows", "sub"))),
        check_vma=False,
    )
```
